32 devices in a mesh: patch: 8 (over z, y), level: 4 (over x, core).
Axes of the slice: x: 2, y: 2, z: 4, core: 2. Of those that a mesh axis runs over, the one named last changes fastest.
Arguments:
- fields: float32 [6, 64, 8192], P(None, None, ('patch', 'level')), may hold values from -6 to 6
- inv_jacobian: float32 [8192], P(('patch', 'level')), may hold values from 0.5 to 2
- diff_matrix: float32 [3, 64, 64], replicated, may hold values from -0.75 to 0.75
- face_interp: float32 [6, 16, 64], replicated, may hold values from -0.75 to 0.75
- lift_matrix: float32 [6, 64, 16], replicated, may hold values from -1.5 to 1.5
- flux_couple: float32 [6, 6, 6], replicated, may hold values from -2.5 to 2.5
- neighbours: int32 [6, 8192], P(None, ('patch', 'level')), may hold values from 0 to 287
- send_index: int32 [2, 512], P(None, ('patch', 'level')), may hold values from 0 to 255
- bound_coef: float32 [6], replicated, may hold values from 0.5 to 1.5
- current_coef: float32 [6], replicated, may hold values from -1 to 1
- time_interp: float32 [64], replicated, may hold values from -2 to 2
- current_history: bfloat16 [64, 4096], P(None, ('patch', 'level')), may hold values from -6 to 6
- group_weight: bfloat16 [32, 4096], P(None, ('patch', 'level')), may hold values from -0.1875 to 0.1875
- projection: bfloat16 [4096, 512], P(('patch', 'level')), may hold values from -6 to 6
- kernels: bfloat16 [4, 8, 4, 64], P('level', 'patch'), may hold values from -0.75 to 0.75
- pair_dest: int32 [4, 8, 4], P('level', 'patch'), may hold values from 0 to 7, as said below
- pair_count: int32 [4, 8], P('level', 'patch'), may hold values from 2 to 4
Outputs:
- field_rate: float32 [6, 64, 8192], P(None, None, ('patch', 'level'))
- boundary_field: float32 [64, 4096], P(None, ('patch', 'level'))
The draws below stay inside these ranges and needn't reach their ends.
Inputs may be any that keep to these rules, and one draw needn't show every extreme that they name: `pair_dest`: in each row the 4 entries are distinct patches, none the row's own patch. Only the first pair_count slots of a group are live. `neighbours`: indices below 256 are the device's own elements, then 16 ghosts from the device below and 16 from the device above along patch+level, wrapping. `send_index`: local element indices of the device.
All inputs are finite; a program needn't handle non-finite values.
Results may differ from the reference program's by a relative error of at most 0.0049.
Values may be sent and summed in bfloat16 or wider, within the bound.
A program may use at most 192 MiB of HBM per device.

```python
import math
import jax
import jax.numpy as jnp
from jax import lax

NP = 64
NFP = 16
BE = 8
E_DEV = 256
HALO = 16
NT = 64
NDIR = 512
B_DEV = 128
GROUPS = 32
PAIRS = 4
ELEMS = 8192
BASIS = 4096
N_PATCH = 8
N_LEVEL = 4
DEVICES = 32


def draw_pair_dest(key, part):
    scores = jax.random.randint(key, (N_LEVEL, N_PATCH, N_PATCH - 1), 0, 1048576)
    scores = scores * N_PATCH + jnp.arange(N_PATCH - 1)[None, None, :]
    order = jnp.argsort(scores, axis=-1, stable=True).astype(jnp.int32)
    offsets = order[:, :, :PAIRS] + 1
    anchor = jnp.arange(N_PATCH, dtype=jnp.int32)[None, :, None]
    return ((anchor + offsets) % N_PATCH).astype(jnp.int32)


def plant(values, stream_key, least, top_value):
    index_at = [jax.random.randint(jax.random.fold_in(stream_key, axis), (), 0, length) for axis, length in enumerate(values.shape)]
    main_axis = values.shape.index(max(values.shape))
    beside = index_at[:main_axis] + [(index_at[main_axis] + 1) % values.shape[main_axis]] + index_at[main_axis + 1:]
    return values.at[tuple(index_at)].set(least).at[tuple(beside)].set(top_value)


def spiked(drawn, key, source, target, blocks, factor):
    owner, partner = [(jnp.arange(drawn.shape[axis_at]) // (drawn.shape[axis_at] // blocks)).reshape([-1 if axis == axis_at else 1 for axis in range(drawn.ndim)]) for axis_at in (source, target)]
    chosen = jax.random.permutation(key, blocks)[partner]
    strong = (owner == chosen) | (owner == (partner + blocks // 2) % blocks)
    return jnp.where(strong, factor * drawn, drawn)


def shard_levels(own_key, extent, shards, least, high):
    gain = 1.0
    for dim, shards_of in shards:
        draws = jax.random.uniform(jax.random.fold_in(jax.random.fold_in(own_key, 6), dim), (shards_of,), jnp.float32, least / len(shards), high / len(shards))
        gain = gain * jnp.repeat(jnp.exp(draws), extent[dim] // shards_of).reshape((-1,) + (1,) * (len(extent) - 1 - dim))
    return gain


def normal_values(stream_key, shape, deviation, most, shards=(), held_as=jnp.bfloat16):
    entries = jax.random.normal(stream_key, shape, jnp.float32) * deviation
    if len(shards) > 0:
        entries = shard_levels(stream_key, shape, shards, -0.22, 0.18) * entries
    return jnp.clip(entries, min=-most, max=most).astype(held_as)


def gaussian_with(key, dims, width, reach, split, heavy, kind=jnp.bfloat16):
    values = width * jax.random.normal(key, dims, jnp.float32)
    if split:
        values = values * shard_levels(key, dims, split, -0.22, 0.18)
    return jnp.clip(spiked(values, jax.random.fold_in(key, 3), *heavy), -reach, reach).astype(kind)


def setup_inputs(seed: int = 0) -> dict:
    arg_keys = jax.random.split(jax.random.key(seed), 18)
    fields = normal_values(arg_keys[0], (6, NP, ELEMS), 1.0, 6.0, ((2, 32),), jnp.float32)
    inv_jacobian = jnp.clip(jnp.exp(math.log(2.0) - 1.3862944 * jax.random.uniform(arg_keys[1], (ELEMS,), jnp.float32) ** shard_levels(arg_keys[1], (ELEMS,), ((0, 32),), -0.2, 0.2)), 0.5, 2.0)
    diff_matrix = normal_values(arg_keys[2], (3, NP, NP), NP ** -0.5, 0.75, (), jnp.float32)
    face_interp = normal_values(arg_keys[3], (6, NFP, NP), NP ** -0.5, 0.75, (), jnp.float32)
    lift_matrix = normal_values(arg_keys[4], (6, NP, NFP), NFP ** -0.5, 1.5, (), jnp.float32)
    flux_couple = normal_values(arg_keys[5], (6, 6, 6), 6 ** -0.5, 2.5, (), jnp.float32)
    neighbours = plant(jax.random.randint(arg_keys[6], (6, ELEMS), 0, E_DEV + 2 * HALO), jax.random.fold_in(arg_keys[6], 1), 0, (E_DEV + 2 * HALO) - 1).astype(jnp.int32)
    send_index = plant(jax.random.randint(arg_keys[7], (2, HALO * DEVICES), 0, E_DEV), jax.random.fold_in(arg_keys[7], 1), 0, E_DEV - 1).astype(jnp.int32)
    bound_coef = jnp.clip(jax.random.uniform(arg_keys[8], (6,), jnp.float32, 0.5, 1.5), 0.5, 1.5)
    current_coef = jnp.clip(jax.random.uniform(arg_keys[9], (6,), jnp.float32, -1.0, 1.0), -1.0, 1.0)
    time_interp = normal_values(arg_keys[10], (NT,), 8 ** -0.5, 2.0, (), jnp.float32)
    current_history = normal_values(arg_keys[11], (NT, BASIS), 1.0, 6.0, ((1, 32),))
    group_weight = gaussian_with(arg_keys[12], (GROUPS, BASIS), BASIS ** -0.5, 0.1875, ((1, 32),), (1, 0, 32, 2.75))
    projection = normal_values(arg_keys[13], (BASIS, NDIR), 1.0, 6.0, ((0, 32),))
    kernels = normal_values(arg_keys[14], (N_LEVEL, N_PATCH, PAIRS, NT), NT ** -0.5, 0.75, ((0, 4), (1, 8)))
    pair_dest = draw_pair_dest(jax.random.fold_in(arg_keys[17], 71), 0)
    pair_count = plant(jax.random.randint(arg_keys[16], (N_LEVEL, N_PATCH), PAIRS // 2, PAIRS + 1), jax.random.fold_in(arg_keys[16], 1), PAIRS // 2, PAIRS).astype(jnp.int32)
    return dict(fields=fields, inv_jacobian=inv_jacobian, diff_matrix=diff_matrix, face_interp=face_interp, lift_matrix=lift_matrix, flux_couple=flux_couple, neighbours=neighbours, send_index=send_index, bound_coef=bound_coef, current_coef=current_coef, time_interp=time_interp, current_history=current_history, group_weight=group_weight, projection=projection, kernels=kernels, pair_dest=pair_dest, pair_count=pair_count)


HIGH = lax.Precision.HIGHEST

def toeplitz(rows):
    count = rows.shape[-1]
    lagged = jnp.arange(count)[:, None] - jnp.arange(count)[None, :]
    picked = jnp.take(rows, jnp.clip(lagged, 0, count - 1), axis=-1)
    return jnp.where(lagged >= 0, picked, jnp.zeros_like(picked))

def own_traces(face_interp, local):
    return jnp.einsum('fqn,cne->fcqe', face_interp, local, precision=HIGH)

def element_rate(local, pool, scale, links, exterior, face_interp, lift_matrix, flux_couple, diff_matrix, own):
    opposite = face_interp[jnp.array([1, 0, 3, 2, 5, 4])]
    across = pool[:, :, links]
    neighbour = jnp.einsum('fqn,cnfe->fcqe', opposite, across, precision=HIGH)
    padded = jnp.pad(exterior, ((0, 0), (0, 0), (0, local.shape[2] - exterior.shape[2])))
    isbound = (jnp.arange(6)[:, None, None, None] == 5) & (jnp.arange(local.shape[2])[None, None, None, :] < BE)
    neighbour = jnp.where(isbound, padded[None], neighbour)
    flux = jnp.einsum('fcd,fdqe->fcqe', flux_couple, neighbour - own, precision=HIGH)
    surface = jnp.einsum('fnq,fcqe->cne', lift_matrix, flux, precision=HIGH)
    grads = jnp.einsum('rmn,cne->rcme', diff_matrix, local, precision=HIGH) * scale
    electric = jnp.stack([grads[1, 5] - grads[2, 4], grads[2, 3] - grads[0, 5], grads[0, 4] - grads[1, 3]])
    magnetic = -jnp.stack([grads[1, 2] - grads[2, 1], grads[2, 0] - grads[0, 2], grads[0, 1] - grads[1, 0]])
    return jnp.concatenate([electric, magnetic], axis=0) + surface

def reference(fields, inv_jacobian, diff_matrix, face_interp, lift_matrix, flux_couple, neighbours, send_index, bound_coef, current_coef, time_interp, current_history, group_weight, projection, kernels, pair_dest, pair_count):
    devices = N_PATCH * N_LEVEL
    local = fields.reshape(6, NP, devices, E_DEV).transpose(2, 0, 1, 3)
    listed = send_index.reshape(2, devices, HALO).transpose(1, 0, 2).reshape(devices, 2 * HALO)
    packed = jax.vmap(lambda block, index: block[:, :, index])(local, listed)
    lower = jnp.roll(packed, 1, axis=0)[..., HALO:]
    upper = jnp.roll(packed, -1, axis=0)[..., :HALO]
    pool = jnp.concatenate([local, lower, upper], axis=-1)
    links = neighbours.reshape(6, devices, E_DEV).transpose(1, 0, 2)
    scales = inv_jacobian.reshape(devices, E_DEV)
    own = jax.vmap(lambda block: own_traces(face_interp, block))(local)
    newest = jnp.einsum('c,dcqe->deq', current_coef, own[:, 5, :, :, :BE], precision=HIGH)
    newest = newest.reshape(1, devices * B_DEV).astype(jnp.bfloat16)
    currents = jnp.concatenate([current_history[1:], newest], axis=0)

    def one_group(row):
        weighted = (currents.astype(jnp.float32) * row.astype(jnp.float32)[None, :]).astype(jnp.bfloat16)
        return jnp.dot(weighted, projection, preferred_element_type=jnp.float32).astype(jnp.bfloat16)
    rays = lax.map(one_group, group_weight)
    live = jnp.arange(PAIRS)[None, None, :] < pair_count[:, :, None]
    slots = (pair_dest[:, :, None, :] == jnp.arange(N_PATCH)[None, None, :, None]) & live[:, :, None, :]
    table = jnp.einsum('lpqj,lpjt->lpqt', slots.astype(jnp.float32), kernels.astype(jnp.float32), precision=HIGH)
    blocks = toeplitz(table)
    sources = rays.reshape(N_PATCH, N_LEVEL, NT, NDIR).transpose(1, 0, 2, 3).astype(jnp.float32)
    incoming = jnp.einsum('lpqts,lpsk->lqtk', blocks, sources, precision=HIGH)
    incoming = incoming.transpose(1, 0, 2, 3).reshape(devices, NT, NDIR).astype(jnp.bfloat16)

    def add_group(total, pair):
        block, row = pair
        image = jnp.dot(block, projection.T, preferred_element_type=jnp.float32)
        return (total + image * row.astype(jnp.float32)[None, :], None)
    start = jnp.zeros((NT, devices * B_DEV), jnp.float32)
    boundary_field, _ = lax.scan(add_group, start, (incoming, group_weight))
    boundary_field = boundary_field * (1.0 / jnp.sqrt(jnp.float32(NDIR)))
    interp = jnp.dot(time_interp, boundary_field, precision=HIGH).reshape(devices, BE, NFP)
    exterior = bound_coef[None, :, None, None] * interp.transpose(0, 2, 1)[:, None]
    rates = jax.vmap(lambda a, b, c, d, e, f: element_rate(a, b, c, d, e, face_interp, lift_matrix, flux_couple, diff_matrix, f))(local, pool, scales, links, exterior, own)
    field_rate = rates.transpose(1, 2, 0, 3).reshape(6, NP, devices * E_DEV)
    return (field_rate, boundary_field)
```

```python
import functools
import math

import jax
import jax.numpy as jnp
from jax import lax
from jax.experimental import pallas as pl
from jax.experimental.pallas import tpu as pltpu
from jax.sharding import PartitionSpec as P

MESH = pl.DeviceIdType.MESH
F32 = jnp.float32
BF16 = jnp.bfloat16
HIGH = lax.Precision.HIGHEST
COLUMNS = 2
CORES = 2


def iota(shape, dim):
    return lax.broadcasted_iota(jnp.int32, shape, dim)


def dot(a, b):
    return jnp.dot(a, b, preferred_element_type=F32)


def split(x):
    high = x.astype(BF16)
    return high, (x - high.astype(F32)).astype(BF16)


def one_hot(mask):
    return jnp.where(mask, 1.0, 0.0).astype(BF16)


def kernel(
    patches,
    levels,
    meta_rows,
    fields,
    scale,
    interp,
    diff,
    lift,
    couple,
    links,
    listed,
    bound_coef,
    current_coef,
    time_interp,
    history,
    weights,
    proj,
    kernels,
    dest,
    count,
    rate,
    boundary,
    pbuf,
    sbuf,
    sib_proj,
    sib_small,
    meta,
    outgoing,
    ghosts,
    pool,
    traces,
    grads,
    flux,
    rsum,
    gains,
    toep,
    gwf,
    partial,
    arrived,
    p_send,
    p_recv,
    s_send,
    s_recv,
    x_send,
    x_recv,
):
    depth = patches // COLUMNS
    wide = levels // CORES
    p, l = lax.axis_index("patch"), lax.axis_index("level")
    z, y = p // COLUMNS, p % COLUMNS
    x, core = l // CORES, l % CORES
    nt = history.shape[0]
    groups, nb = weights.shape
    pairs = kernels.shape[0]
    faces, nodes, elements = fields.shape
    halo = listed.shape[1]
    nq = interp.shape[0] // faces
    bound = nb // nq
    me = p * levels + l
    everyone = patches * levels

    def ident(flat):
        return (flat // levels, flat % levels)

    sibling = (p, x * CORES + (1 - core))
    after = ident((me + 1) % everyone)
    before = ident((me + everyone - 1) % everyone)
    ya, xa = (y + 1 - core) % COLUMNS, (x + core) % wide
    yb, xb = (y + core) % COLUMNS, (x + 1 - core) % wide
    near = (z * COLUMNS + ya, xa * CORES + core)
    far = (z * COLUMNS + yb, xb * CORES + core)

    def column(step):
        return ((z + step) % depth * COLUMNS + y, l)

    barrier = pltpu.get_barrier_semaphore()
    partners = [sibling, near, far, after, before] + [column(k) for k in range(1, depth)]
    for other in partners:
        pl.semaphore_signal(barrier, inc=1, device_id=other, device_id_type=MESH)

    mine = p * wide + x
    pbuf[mine] = proj[...]

    kr = dot(kernels[...], one_hot(iota((nt, 128), 0) + iota((nt, 128), 1) == nt - 1))
    row = iota((meta_rows, 128), 0)
    lane = iota((meta_rows, 128), 1)
    held = kr
    if meta_rows > pairs:
        held = jnp.concatenate([kr, jnp.zeros((meta_rows - pairs, 128), F32)], axis=0)
    goal = jnp.zeros((meta_rows, 128), F32)
    for j in range(pairs):
        goal = jnp.where(row == j, dest[j].astype(F32), goal)
    held = jnp.where(row < count[0], held, 0.0)
    meta[0:meta_rows] = jnp.where(lane < nt, held, goal).astype(BF16)
    meta[meta_rows:] = weights[...]

    mixed = current_coef[0] * fields[0, :, 0:128]
    for c in range(1, faces):
        mixed += current_coef[c] * fields[c, :, 0:128]
    last = jnp.dot(interp[nq * (faces - 1) :, :], mixed, precision=HIGH, preferred_element_type=F32)
    spread = jnp.where(iota((128, nb), 0) == iota((128, nb), 1) // nq, 1.0, 0.0)
    last = jnp.dot(last, spread, precision=HIGH, preferred_element_type=F32)
    diagonal = iota((nq, nb), 0) == iota((nq, nb), 1) % nq
    newest = jnp.sum(jnp.where(diagonal, last, 0.0), axis=0, keepdims=True)
    moved = pltpu.roll(history[...].astype(F32), nt - 1, 0)
    currents = jnp.where(iota((nt, nb), 0) == nt - 1, newest, moved).astype(BF16)
    sbuf[mine, 0:nt] = currents
    sbuf[mine, nt : nt + groups] = weights[...]
    base = nt + groups
    sbuf[mine, base : base + meta_rows] = meta[0:meta_rows]

    pl.semaphore_wait(barrier, len(partners))

    sends = []

    def send(src, dst, s_sem, r_sem, other):
        copy = pltpu.make_async_remote_copy(
            src_ref=src, dst_ref=dst, send_sem=s_sem, recv_sem=r_sem,
            device_id=other, device_id_type=MESH,
        )
        copy.start()
        sends.append(copy)
        return copy

    slots = [0, 0]

    def send_p(slot, other):
        i = slots[0]
        slots[0] += 1
        send(pbuf.at[slot], pbuf.at[slot], p_send.at[i], p_recv.at[slot], other)

    def send_s(slot, other):
        i = slots[1]
        slots[1] += 1
        send(sbuf.at[slot], sbuf.at[slot], s_send.at[i], s_recv.at[slot], other)

    def wait_p(slot):
        pltpu.make_async_copy(pbuf.at[slot], pbuf.at[slot], p_recv.at[slot]).wait()

    def wait_s(slot):
        pltpu.make_async_copy(sbuf.at[slot], sbuf.at[slot], s_recv.at[slot]).wait()

    sib_meta = send(meta, sib_small, x_send.at[0], x_recv.at[0], sibling)
    send_p(mine, far)
    send_p(mine, near)
    for k in range(1, depth):
        send_p(mine, column(k))
    sib_copy = send(proj, sib_proj, x_send.at[1], x_recv.at[1], sibling)

    place = jnp.where(iota((halo, 128), 0) == iota((halo, 128), 1) % halo, 1.0, 0.0)
    wanted = jnp.dot(listed[...].astype(F32), place, precision=HIGH, preferred_element_type=F32)
    wanted = wanted.astype(jnp.int32)
    picks = jnp.concatenate(
        [one_hot(iota((elements, 128), 0) == wanted[r : r + 1, :]) for r in range(2)], axis=1
    )
    sent = jnp.zeros((nodes, 256), F32)
    which = iota((nodes, 256), 1) % 128 // halo
    for c in range(faces):
        sent = jnp.where(which == c, dot(fields[c].astype(BF16), picks), sent)
    outgoing[0] = sent[:, 0:128].astype(BF16)
    outgoing[1] = sent[:, 128:256].astype(BF16)

    sib_meta.wait_recv()
    sbuf[mine, base + meta_rows : base + 2 * meta_rows] = sib_small[0:meta_rows]
    send_s(mine, far)
    send_s(mine, near)
    for k in range(1, depth):
        send_s(mine, column(k))
    up = send(outgoing.at[1], ghosts.at[0], x_send.at[2], x_recv.at[2], after)
    down = send(outgoing.at[0], ghosts.at[1], x_send.at[3], x_recv.at[3], before)

    rsum[...] = jnp.zeros_like(rsum)

    def slot_of(zz, yy, xx):
        return (zz * COLUMNS + yy) * wide + xx

    def prepare(slot):
        info = sbuf[slot, base : base + 2 * meta_rows].astype(F32)
        rows = iota((2 * meta_rows, groups), 0)
        theirs = jnp.where(rows < meta_rows, core, 1 - core)
        target = (info[:, nt : nt + 1].astype(jnp.int32)) * levels + slot % wide * CORES + theirs
        picked = one_hot(iota((2 * meta_rows, groups), 1) == target)
        both = jnp.concatenate([weights[...], sib_small[meta_rows:]], axis=1)
        gains[slot] = dot(picked, both)
        first = iota((nt, 128), 1) < nt
        for k in range(2):
            for j in range(0, pairs, 2):
                rolled = []
                for i in range(2):
                    r = k * meta_rows + j + i
                    line = jnp.where(iota((1, 128), 1) < nt, info[r : r + 1, :], 0.0)
                    line = jnp.broadcast_to(line, (nt, 128))
                    rolled.append(
                        pltpu.roll(line, (128 - nt + 1 + nt * i) % 128, 1, stride=1, stride_axis=0)
                    )
                at = (k * pairs + j) * nt
                toep[slot, :, at : at + 128] = jnp.where(first, rolled[0], rolled[1]).astype(BF16)

    def absorb(one, two):
        chip = jnp.concatenate([proj[...], sib_proj[...]], axis=0)
        both = []
        for i, slot in enumerate((one, two)):
            prepare(slot)
            s = lax.dot_general(
                pbuf[slot], chip, (((1,), (1,)), ((), ())), preferred_element_type=F32
            )
            both.append(s.astype(BF16))
            gwf[i] = sbuf[slot, nt : nt + groups].astype(F32)
        s = jnp.concatenate(both, axis=0)
        cur = [sbuf[slot, 0:nt].astype(F32) for slot in (one, two)]

        def chunk(i, carry):
            at = pl.multiple_of(i * 8, 8)
            w = [gwf[i2, pl.ds(at, 8), :] for i2 in range(2)]
            lhs = jnp.concatenate(
                [
                    jnp.concatenate(
                        [(cur[i2] * w[i2][g : g + 1, :]).astype(BF16) for i2 in range(2)], axis=1
                    )
                    for g in range(8)
                ],
                axis=0,
            )
            rows = pl.ds(pl.multiple_of(i * 8 * nt, 8 * nt), 8 * nt)
            rsum[rows, :] += dot(lhs, s)
            return carry

        lax.fori_loop(0, groups // 8, chunk, 0)

    home = [slot_of((z + depth - k) % depth, y, x) for k in range(depth)]
    for slot in home[1:]:
        wait_p(slot)
        send_p(slot, far)
        send_p(slot, near)
        wait_s(slot)
        send_s(slot, far)
        send_s(slot, near)

    up.wait_recv()
    down.wait_recv()
    arrivals = jnp.concatenate([ghosts[0], ghosts[1]], axis=1)
    r_i = iota((256, faces * 128), 0)
    m_i = iota((256, faces * 128), 1)
    lands = (r_i // 128 == m_i % 128 // halo) & (r_i % 128 == m_i // 128 * halo + m_i % halo)
    lands = one_hot(lands)
    unpacked = dot(arrivals, lands)
    width = elements + 128
    w_all = jnp.concatenate([interp[...], diff[...]], axis=0)
    w_hi, w_lo = split(w_all)
    w3 = jnp.concatenate([w_hi, w_hi, w_lo], axis=1)
    nf = faces * nq
    for c in range(faces):
        xc = jnp.concatenate([fields[c], unpacked[:, c * 128 : (c + 1) * 128]], axis=1)
        hi, lo = split(xc)
        got = dot(w3, jnp.concatenate([hi, lo, hi], axis=0))
        traces[c] = got[0:nf]
        grads[c] = got[nf:, 0:elements] * scale[...]

    nears = [slot_of((z + depth - k) % depth, ya, xa) for k in range(depth)]

    def forward(slot):
        wait_p(slot)
        send_p(slot, far)
        wait_s(slot)
        send_s(slot, far)

    todo = list(nears)
    lane_e = iota((nq, elements), 1)
    for f in range(faces):
        o = f + 1 - 2 * (f % 2)
        block = jnp.concatenate([traces[c, o * nq : (o + 1) * nq, :] for c in range(faces)], axis=0)
        hi, lo = split(block)
        pick = one_hot(iota((width, elements), 0) == links[f : f + 1, :])
        got = dot(jnp.concatenate([hi, lo], axis=0), pick)
        jump = []
        for c in range(faces):
            nbr = got[c * nq : (c + 1) * nq] + got[nf + c * nq : nf + (c + 1) * nq]
            if f == faces - 1:
                nbr = jnp.where(lane_e < bound, 0.0, nbr)
            jump.append(nbr - traces[c, f * nq : (f + 1) * nq, 0:elements])
        for c in range(faces):
            total = couple[(f * faces + c) * faces] * jump[0]
            for d in range(1, faces):
                total += couple[(f * faces + c) * faces + d] * jump[d]
            flux[c, f * nq : (f + 1) * nq, :] = total
    for slot in todo:
        forward(slot)

    sib_copy.wait_recv()
    l_hi = jnp.zeros((nodes, 128), F32)
    l_lo = jnp.zeros((nodes, 128), F32)
    for f in range(faces):
        hi, lo = split(lift[f])
        here = one_hot(iota((nq, 128), 1) == iota((nq, 128), 0) + f * nq)
        l_hi += dot(hi, here)
        l_lo += dot(lo, here)
    l_hi, l_lo = l_hi.astype(BF16), l_lo.astype(BF16)
    l3 = jnp.concatenate([l_hi, l_hi, l_lo], axis=1)
    empty = jnp.zeros((128 - nf, elements), BF16)
    for c in range(faces):
        hi, lo = split(flux[c])
        hi = jnp.concatenate([hi, empty], axis=0)
        lo = jnp.concatenate([lo, empty], axis=0)
        surface = dot(l3, jnp.concatenate([hi, lo, hi], axis=0))
        i, j = (c + 1) % 3, (c + 2) % 3
        other = 3 - c // 3 * 3

        def grad(r, d):
            return grads[d, r * nodes : (r + 1) * nodes, :]

        curl = grad(i, other + j) - grad(j, other + i)
        rate[c] = surface + curl if c < 3 else surface - curl

    for k in range(0, depth, 2):
        absorb(home[k], home[k + 1])
    for k in range(0, depth, 2):
        absorb(nears[k], nears[k + 1])
    ends = [slot_of((z + depth - k) % depth, yb, xb) for k in range(depth)]
    ends += [slot_of((z + depth - k) % depth, (y + 1) % COLUMNS, (x + 1) % wide) for k in range(depth)]
    for k in range(0, 2 * depth, 2):
        for slot in ends[k : k + 2]:
            wait_p(slot)
            wait_s(slot)
        absorb(ends[k], ends[k + 1])

    def finish(slot, total):
        parts = []
        for k in range(2):
            g = slot * 2 + (core if k == 0 else 1 - core)
            r = rsum[pl.ds(pl.multiple_of(g * nt, nt), nt), :]
            for j in range(pairs):
                gain = gains[slot, k * meta_rows + j : k * meta_rows + j + 1, :]
                parts.append((r * gain).astype(BF16))
        return total + dot(toep[slot], jnp.concatenate(parts, axis=0))

    total = lax.fori_loop(0, patches * wide, finish, jnp.zeros((nt, 2 * nb), F32))
    partial[...] = total[:, nb:]
    swap = send(partial, arrived, x_send.at[4], x_recv.at[4], sibling)
    swap.wait_recv()
    field = (total[:, 0:nb] + arrived[...]) * (1.0 / math.sqrt(proj.shape[1]))
    boundary[...] = field

    seen = jnp.dot(time_interp[...], field, precision=HIGH, preferred_element_type=F32)
    seen = jnp.where(diagonal, jnp.broadcast_to(seen, (nq, nb)), 0.0)
    gather = jnp.where(iota((nb, 128), 0) // nq == iota((nb, 128), 1), 1.0, 0.0)
    seen = jnp.dot(seen, gather, precision=HIGH, preferred_element_type=F32)
    added = jnp.dot(lift[faces - 1], seen, precision=HIGH, preferred_element_type=F32)
    for c in range(faces):
        factor = couple[((faces - 1) * faces + c) * faces] * bound_coef[0]
        for d in range(1, faces):
            factor += couple[((faces - 1) * faces + c) * faces + d] * bound_coef[d]
        rate[c, :, 0:128] += factor * added

    for copy in sends:
        copy.wait_send()


def per_device(
    fields, inv_jacobian, diff_matrix, face_interp, lift_matrix, flux_couple, neighbours,
    send_index, bound_coef, current_coef, time_interp, current_history, group_weight,
    projection, kernels, pair_dest, pair_count,
):
    patches, levels = lax.axis_size("patch"), lax.axis_size("level")
    faces, nodes, elements = fields.shape
    nt, nb = current_history.shape
    groups = group_weight.shape[0]
    ndir = projection.shape[1]
    pairs = kernels.shape[2]
    meta_rows = -(-pairs // 16) * 16
    nq = face_interp.shape[1]
    chips = patches * (levels // CORES)
    depth = patches // COLUMNS
    n_send = 4 * depth - 1
    rows = nt + groups + 2 * meta_rows
    vmem = pl.BlockSpec(memory_space=pltpu.VMEM)
    smem = pl.BlockSpec(memory_space=pltpu.SMEM)
    dma = pltpu.SemaphoreType.DMA
    return pl.pallas_call(
        functools.partial(kernel, patches, levels, meta_rows),
        out_shape=(
            jax.ShapeDtypeStruct(fields.shape, F32),
            jax.ShapeDtypeStruct((nt, nb), F32),
        ),
        in_specs=[vmem] * 5 + [smem] + [vmem] * 2 + [smem] * 2 + [vmem] * 5 + [smem] * 2,
        out_specs=(vmem, vmem),
        scratch_shapes=[
            pltpu.VMEM((chips, nb, ndir), BF16),
            pltpu.VMEM((chips, rows, nb), BF16),
            pltpu.VMEM((nb, ndir), BF16),
            pltpu.VMEM((meta_rows + groups, nb), BF16),
            pltpu.VMEM((meta_rows + groups, nb), BF16),
            pltpu.VMEM((2, nodes, 128), BF16),
            pltpu.VMEM((2, nodes, 128), BF16),
            pltpu.VMEM((8, 128), F32),
            pltpu.VMEM((faces, faces * nq, elements + 128), F32),
            pltpu.VMEM((faces, 3 * nodes, elements), F32),
            pltpu.VMEM((faces, faces * nq, elements), F32),
            pltpu.VMEM((groups * nt, 2 * nb), F32),
            pltpu.VMEM((chips, 2 * meta_rows, 2 * nb), F32),
            pltpu.VMEM((chips, nt, 2 * pairs * nt), BF16),
            pltpu.VMEM((2, groups, nb), F32),
            pltpu.VMEM((nt, nb), F32),
            pltpu.VMEM((nt, nb), F32),
            dma((n_send,)),
            dma((chips,)),
            dma((n_send,)),
            dma((chips,)),
            dma((5,)),
            dma((5,)),
        ],
        compiler_params=pltpu.CompilerParams(
            collective_id=0, has_side_effects=True, vmem_limit_bytes=56 * 1024 * 1024
        ),
    )(
        fields,
        inv_jacobian.reshape(1, elements),
        face_interp.reshape(faces * nq, nodes),
        diff_matrix.reshape(3 * nodes, nodes),
        lift_matrix,
        flux_couple.reshape(-1),
        neighbours,
        send_index,
        bound_coef,
        current_coef,
        time_interp.reshape(1, nt),
        current_history,
        group_weight,
        projection,
        kernels.reshape(pairs, nt),
        pair_dest.reshape(pairs),
        pair_count.reshape(1),
    )


def solution(mesh):
    both = ("patch", "level")
    placed = (
        P(None, None, both),
        P(both),
        P(),
        P(),
        P(),
        P(),
        P(None, both),
        P(None, both),
        P(),
        P(),
        P(),
        P(None, both),
        P(None, both),
        P(both, None),
        P("level", "patch", None, None),
        P("level", "patch", None),
        P("level", "patch"),
    )
    return jax.shard_map(
        per_device,
        mesh=mesh,
        in_specs=placed,
        out_specs=(P(None, None, both), P(None, both)),
        check_vma=False,
    )
```

```python
import functools
import math

import jax
import jax.numpy as jnp
from jax import lax
from jax.experimental import pallas as pl
from jax.experimental.pallas import tpu as pltpu
from jax.sharding import PartitionSpec as P

MESH = pl.DeviceIdType.MESH
F32 = jnp.float32
BF16 = jnp.bfloat16
HIGH = lax.Precision.HIGHEST
COLUMNS = 2
CORES = 2


def iota(shape, dim):
    return lax.broadcasted_iota(jnp.int32, shape, dim)


def dot(a, b):
    return jnp.dot(a, b, preferred_element_type=F32)


def split(x):
    high = x.astype(BF16)
    return high, (x - high.astype(F32)).astype(BF16)


def one_hot(mask):
    return jnp.where(mask, 1.0, 0.0).astype(BF16)


def kernel(
    patches,
    levels,
    meta_rows,
    fields,
    scale,
    interp,
    diff,
    lift,
    couple,
    links,
    listed,
    bound_coef,
    current_coef,
    time_interp,
    history,
    weights,
    proj,
    kernels,
    dest,
    count,
    rate,
    boundary,
    pbuf,
    sbuf,
    chip,
    sib_small,
    meta,
    outgoing,
    ghosts,
    pool,
    traces,
    grads,
    flux,
    rsum,
    gains,
    toep,
    gwf,
    partial,
    arrived,
    p_send,
    p_recv,
    s_send,
    s_recv,
    x_send,
    x_recv,
):
    depth = patches // COLUMNS
    wide = levels // CORES
    p, l = lax.axis_index("patch"), lax.axis_index("level")
    z, y = p // COLUMNS, p % COLUMNS
    x, core = l // CORES, l % CORES
    nt = history.shape[0]
    groups, nb = weights.shape
    pairs = kernels.shape[0]
    faces, nodes, elements = fields.shape
    halo = listed.shape[1]
    nq = interp.shape[0] // faces
    bound = nb // nq
    me = p * levels + l
    everyone = patches * levels

    def ident(flat):
        return (flat // levels, flat % levels)

    sibling = (p, x * CORES + (1 - core))
    after = ident((me + 1) % everyone)
    before = ident((me + everyone - 1) % everyone)
    ya, xa = (y + 1 - core) % COLUMNS, (x + core) % wide
    yb, xb = (y + core) % COLUMNS, (x + 1 - core) % wide
    near = (z * COLUMNS + ya, xa * CORES + core)
    far = (z * COLUMNS + yb, xb * CORES + core)

    above = ((z + 1) % depth * COLUMNS + y, l)
    below = ((z + depth - 1) % depth * COLUMNS + y, l)
    has_above, has_below = z < depth - 1, z > 0

    barrier = pltpu.get_barrier_semaphore()

    def greet(other):
        pl.semaphore_signal(barrier, inc=1, device_id=other, device_id_type=MESH)

    partners = [sibling, near, far, after, before, above, below]
    for other in partners:
        greet(other)
    pl.semaphore_wait(barrier, len(partners))

    sends = []

    def remote(src, dst, s_sem, r_sem, other):
        return pltpu.make_async_remote_copy(
            src_ref=src, dst_ref=dst, send_sem=s_sem, recv_sem=r_sem,
            device_id=other, device_id_type=MESH,
        )

    def send(*args):
        copy = remote(*args)
        copy.start()
        sends.append(copy)
        return copy

    mine = p * wide + x

    def slot_of(zz, yy, xx):
        return (zz * COLUMNS + yy) * wide + xx

    def hop(kind, slot, i, other, own=False):
        buf, s_sem, r_sem = (pbuf, p_send, p_recv) if kind == "p" else (sbuf, s_send, s_recv)
        src = proj if own and kind == "p" else buf.at[slot]
        return remote(src, buf.at[slot], s_sem.at[i], r_sem.at[slot], other)

    def wait(kind, slot):
        buf, r_sem = (pbuf, p_recv) if kind == "p" else (sbuf, s_recv)
        pltpu.make_async_copy(buf.at[slot], buf.at[slot], r_sem.at[slot]).wait()

    def hops(kind, zz, k, side, act):
        slot = slot_of(zz, y, x)
        own = k == 0
        if own or side == "below":
            pl.when(has_above)(lambda: act(hop(kind, slot, 3 * depth + k, above, own)))
        if own or side == "above":
            pl.when(has_below)(lambda: act(hop(kind, slot, 4 * depth + k, below, own)))
        act(hop(kind, slot, depth + zz, far, own))
        act(hop(kind, slot, zz, near, own))

    def start(copy):
        copy.start()

    def chain(kind, k, act, receive):
        def from_below():
            if receive:
                wait(kind, slot_of(z - k, y, x))
            hops(kind, z - k, k, "below", act)

        def from_above():
            if receive:
                wait(kind, slot_of(z + k, y, x))
            hops(kind, z + k, k, "above", act)

        pl.when(z >= k)(from_below)
        pl.when(z + k < depth)(from_above)

    hops("p", z, 0, "", start)
    sib_copy = send(proj, chip.at[1], x_send.at[1], x_recv.at[1], sibling)

    kr = dot(kernels[...], one_hot(iota((nt, 128), 0) + iota((nt, 128), 1) == nt - 1))
    row = iota((meta_rows, 128), 0)
    lane = iota((meta_rows, 128), 1)
    held = kr
    if meta_rows > pairs:
        held = jnp.concatenate([kr, jnp.zeros((meta_rows - pairs, 128), F32)], axis=0)
    goal = jnp.zeros((meta_rows, 128), F32)
    for j in range(pairs):
        goal = jnp.where(row == j, dest[j].astype(F32), goal)
    held = jnp.where(row < count[0, 0], held, 0.0)
    meta[0:meta_rows] = jnp.where(lane < nt, held, goal).astype(BF16)
    meta[meta_rows:] = weights[...]

    sib_meta = send(meta, sib_small, x_send.at[0], x_recv.at[0], sibling)
    mixed = current_coef[0] * fields[0, :, 0:128]
    for c in range(1, faces):
        mixed += current_coef[c] * fields[c, :, 0:128]
    last = jnp.dot(interp[nq * (faces - 1) :, :], mixed, precision=HIGH, preferred_element_type=F32)
    spread = jnp.where(iota((128, nb), 0) == iota((128, nb), 1) // nq, 1.0, 0.0)
    last = jnp.dot(last, spread, precision=HIGH, preferred_element_type=F32)
    diagonal = iota((nq, nb), 0) == iota((nq, nb), 1) % nq
    newest = jnp.sum(jnp.where(diagonal, last, 0.0), axis=0, keepdims=True)
    moved = pltpu.roll(history[...].astype(F32), nt - 1, 0)
    currents = jnp.where(iota((nt, nb), 0) == nt - 1, newest, moved).astype(BF16)
    sbuf[mine, 0:nt] = currents
    sbuf[mine, nt : nt + groups] = weights[...]
    base = nt + groups
    sbuf[mine, base : base + meta_rows] = meta[0:meta_rows]

    place = jnp.where(iota((halo, 128), 0) == iota((halo, 128), 1) % halo, 1.0, 0.0)
    wanted = jnp.dot(listed[...].astype(F32), place, precision=HIGH, preferred_element_type=F32)
    wanted = wanted.astype(jnp.int32)
    picks = jnp.concatenate(
        [one_hot(iota((elements, 128), 0) == wanted[r : r + 1, :]) for r in range(2)], axis=1
    )
    sent = jnp.zeros((nodes, 256), F32)
    which = iota((nodes, 256), 1) % 128 // halo
    for c in range(faces):
        sent = jnp.where(which == c, dot(fields[c].astype(BF16), picks), sent)
    outgoing[0] = sent[:, 0:128].astype(BF16)
    outgoing[1] = sent[:, 128:256].astype(BF16)

    sib_meta.wait_recv()
    sbuf[mine, base + meta_rows : base + 2 * meta_rows] = sib_small[0:meta_rows]
    hops("s", z, 0, "", start)
    up = send(outgoing.at[1], ghosts.at[0], x_send.at[2], x_recv.at[2], after)
    down = send(outgoing.at[0], ghosts.at[1], x_send.at[3], x_recv.at[3], before)

    pbuf[mine] = proj[...]
    chip[0] = proj[...]
    rsum[...] = jnp.zeros_like(rsum)

    def prepare(slot):
        info = sbuf[slot, base : base + 2 * meta_rows].astype(F32)
        rows = iota((2 * meta_rows, groups), 0)
        theirs = jnp.where(rows < meta_rows, core, 1 - core)
        target = (info[:, nt : nt + 1].astype(jnp.int32)) * levels + slot % wide * CORES + theirs
        picked = one_hot(iota((2 * meta_rows, groups), 1) == target)
        both = jnp.concatenate([weights[...], sib_small[meta_rows:]], axis=1)
        gains[slot] = dot(picked, both)
        first = iota((nt, 128), 1) < nt
        for k in range(2):
            for j in range(0, pairs, 2):
                rolled = []
                for i in range(2):
                    r = k * meta_rows + j + i
                    line = jnp.where(iota((1, 128), 1) < nt, info[r : r + 1, :], 0.0)
                    line = jnp.broadcast_to(line, (nt, 128))
                    rolled.append(
                        pltpu.roll(line, (128 - nt + 1 + nt * i) % 128, 1, stride=1, stride_axis=0)
                    )
                at = (k * pairs + j) * nt
                toep[slot, :, at : at + 128] = jnp.where(first, rolled[0], rolled[1]).astype(BF16)

    def absorb(slots):
        n = len(slots)
        for i, slot in enumerate(slots):
            prepare(slot)
            gwf[i] = sbuf[slot, nt : nt + groups].astype(F32)
        s = lax.dot_general(
            jnp.concatenate([pbuf[slot] for slot in slots], axis=0),
            chip[...].reshape(2 * nb, proj.shape[1]),
            (((1,), (1,)), ((), ())),
            preferred_element_type=F32,
        ).astype(BF16)
        cur = [sbuf[slot, 0:nt].astype(F32) for slot in slots]

        def chunk(i, carry):
            at = pl.multiple_of(i * 8, 8)
            w = [gwf[j, pl.ds(at, 8), :] for j in range(n)]
            lhs = jnp.concatenate(
                [
                    jnp.concatenate(
                        [(cur[j] * w[j][g : g + 1, :]).astype(BF16) for j in range(n)], axis=1
                    )
                    for g in range(8)
                ],
                axis=0,
            )
            rows = pl.ds(pl.multiple_of(i * 8 * nt, 8 * nt), 8 * nt)
            rsum[rows, :] += dot(lhs, s)
            return carry

        lax.fori_loop(0, groups // 8, chunk, 0)

    home = [slot_of((z + depth - k) % depth, y, x) for k in range(depth)]
    nears = [slot_of((z + depth - k) % depth, ya, xa) for k in range(depth)]
    half = depth // 2

    def forward(k):
        for kind in ("p", "s"):
            wait(kind, nears[k])
            hop(kind, nears[k], 2 * depth + k, far).start()

    for k in range(1, depth):
        chain("p", k, start, True)
        chain("s", k, start, True)
    forward(0)

    up.wait_recv()
    down.wait_recv()
    arrivals = jnp.concatenate([ghosts[0], ghosts[1]], axis=1)
    r_i = iota((256, faces * 128), 0)
    m_i = iota((256, faces * 128), 1)
    lands = (r_i // 128 == m_i % 128 // halo) & (r_i % 128 == m_i // 128 * halo + m_i % halo)
    lands = one_hot(lands)
    unpacked = dot(arrivals, lands)
    width = elements + 128
    w_all = jnp.concatenate([interp[...], diff[...]], axis=0)
    w_hi, w_lo = split(w_all)
    w3 = jnp.concatenate([w_hi, w_hi, w_lo], axis=1)
    nf = faces * nq
    for c in range(faces):
        xc = jnp.concatenate([fields[c], unpacked[:, c * 128 : (c + 1) * 128]], axis=1)
        hi, lo = split(xc)
        got = dot(w3, jnp.concatenate([hi, lo, hi], axis=0))
        traces[c] = got[0:nf]
        grads[c] = got[nf:, 0:elements] * scale[...]

    lane_e = iota((nq, elements), 1)
    for f in range(faces):
        o = f + 1 - 2 * (f % 2)
        block = jnp.concatenate([traces[c, o * nq : (o + 1) * nq, :] for c in range(faces)], axis=0)
        hi, lo = split(block)
        pick = one_hot(iota((width, elements), 0) == links[f : f + 1, :])
        got = dot(jnp.concatenate([hi, lo], axis=0), pick)
        jump = []
        for c in range(faces):
            nbr = got[c * nq : (c + 1) * nq] + got[nf + c * nq : nf + (c + 1) * nq]
            if f == faces - 1:
                nbr = jnp.where(lane_e < bound, 0.0, nbr)
            jump.append(nbr - traces[c, f * nq : (f + 1) * nq, 0:elements])
        for c in range(faces):
            total = couple[f, c : c + 1, 0:1] * jump[0]
            for d in range(1, faces):
                total += couple[f, c : c + 1, d : d + 1] * jump[d]
            flux[c, f * nq : (f + 1) * nq, :] = total
    for k in range(1, half):
        forward(k)
    sib_copy.wait_recv()
    flat = jnp.concatenate([lift[...].reshape(nf, nodes), jnp.zeros((128 - nf, nodes), F32)], axis=0)
    l_hi, l_lo = split(flat.T)
    l3 = jnp.concatenate([l_hi, l_hi, l_lo], axis=1)
    empty = jnp.zeros((128 - nf, elements), BF16)
    for c in range(faces):
        hi, lo = split(flux[c])
        hi = jnp.concatenate([hi, empty], axis=0)
        lo = jnp.concatenate([lo, empty], axis=0)
        surface = dot(l3, jnp.concatenate([hi, lo, hi], axis=0))
        i, j = (c + 1) % 3, (c + 2) % 3
        other = 3 - c // 3 * 3

        def grad(r, d):
            return grads[d, r * nodes : (r + 1) * nodes, :]

        curl = grad(i, other + j) - grad(j, other + i)
        rate[c] = surface + curl if c < 3 else surface - curl

    def some(slots, width):
        for k in range(0, len(slots), width):
            absorb(slots[k : k + width])

    some(home, 4)
    for k in range(half, depth):
        forward(k)
    some(nears, 4)
    ends = [slot_of((z + depth - k) % depth, yb, xb) for k in range(depth)]
    for slot in ends:
        wait("p", slot)
        wait("s", slot)
    some(ends, 4)
    ends = [slot_of((z + depth - k) % depth, (y + 1) % COLUMNS, (x + 1) % wide) for k in range(depth)]
    for k in range(0, depth, 2):
        for slot in ends[k : k + 2]:
            wait("p", slot)
            wait("s", slot)
        absorb(ends[k : k + 2])

    def finish(slot, total):
        parts = []
        for k in range(2):
            g = slot * 2 + (core if k == 0 else 1 - core)
            r = rsum[pl.ds(pl.multiple_of(g * nt, nt), nt), :]
            for j in range(pairs):
                gain = gains[slot, k * meta_rows + j : k * meta_rows + j + 1, :]
                parts.append((r * gain).astype(BF16))
        return total + dot(toep[slot], jnp.concatenate(parts, axis=0))

    total = lax.fori_loop(0, patches * wide, finish, jnp.zeros((nt, 2 * nb), F32), unroll=4)
    partial[...] = total[:, nb:]
    swap = send(partial, arrived, x_send.at[4], x_recv.at[4], sibling)
    swap.wait_recv()
    field = (total[:, 0:nb] + arrived[...]) * (1.0 / math.sqrt(proj.shape[1]))
    boundary[...] = field

    seen = jnp.dot(time_interp[...], field, precision=HIGH, preferred_element_type=F32)
    seen = jnp.where(diagonal, jnp.broadcast_to(seen, (nq, nb)), 0.0)
    gather = jnp.where(iota((nb, 128), 0) // nq == iota((nb, 128), 1), 1.0, 0.0)
    seen = jnp.dot(seen, gather, precision=HIGH, preferred_element_type=F32)
    added = jnp.dot(lift[faces - 1].T, seen, precision=HIGH, preferred_element_type=F32)
    for c in range(faces):
        factor = couple[faces - 1, c : c + 1, 0:1] * bound_coef[0]
        for d in range(1, faces):
            factor += couple[faces - 1, c : c + 1, d : d + 1] * bound_coef[d]
        rate[c, :, 0:128] += factor * added

    for copy in sends:
        copy.wait_send()

    def sent_off(copy):
        copy.wait_send()

    for kind in ("p", "s"):
        hops(kind, z, 0, "", sent_off)
        for k in range(1, depth):
            chain(kind, k, sent_off, False)
        for k in range(depth):
            hop(kind, nears[k], 2 * depth + k, far).wait_send()


def per_device(
    fields, inv_jacobian, diff_matrix, face_interp, lift_matrix, flux_couple, neighbours,
    send_index, bound_coef, current_coef, time_interp, current_history, group_weight,
    projection, kernels, pair_dest, pair_count,
):
    patches, levels = lax.axis_size("patch"), lax.axis_size("level")
    faces, nodes, elements = fields.shape
    nt, nb = current_history.shape
    groups = group_weight.shape[0]
    ndir = projection.shape[1]
    pairs = kernels.shape[2]
    meta_rows = -(-pairs // 16) * 16
    nq = face_interp.shape[1]
    chips = patches * (levels // CORES)
    depth = patches // COLUMNS
    n_send = 5 * depth
    rows = nt + groups + 2 * meta_rows
    vmem = pl.BlockSpec(memory_space=pltpu.VMEM)
    smem = pl.BlockSpec(memory_space=pltpu.SMEM)
    dma = pltpu.SemaphoreType.DMA
    return pl.pallas_call(
        functools.partial(kernel, patches, levels, meta_rows),
        out_shape=(
            jax.ShapeDtypeStruct(fields.shape, F32),
            jax.ShapeDtypeStruct((nt, nb), F32),
        ),
        in_specs=[vmem] * 8 + [smem] * 2 + [vmem] * 5 + [smem] * 2,
        out_specs=(vmem, vmem),
        scratch_shapes=[
            pltpu.VMEM((chips, nb, ndir), BF16),
            pltpu.VMEM((chips, rows, nb), BF16),
            pltpu.VMEM((2, nb, ndir), BF16),
            pltpu.VMEM((meta_rows + groups, nb), BF16),
            pltpu.VMEM((meta_rows + groups, nb), BF16),
            pltpu.VMEM((2, nodes, 128), BF16),
            pltpu.VMEM((2, nodes, 128), BF16),
            pltpu.VMEM((8, 128), F32),
            pltpu.VMEM((faces, faces * nq, elements + 128), F32),
            pltpu.VMEM((faces, 3 * nodes, elements), F32),
            pltpu.VMEM((faces, faces * nq, elements), F32),
            pltpu.VMEM((groups * nt, 2 * nb), F32),
            pltpu.VMEM((chips, 2 * meta_rows, 2 * nb), F32),
            pltpu.VMEM((chips, nt, 2 * pairs * nt), BF16),
            pltpu.VMEM((4, groups, nb), F32),
            pltpu.VMEM((nt, nb), F32),
            pltpu.VMEM((nt, nb), F32),
            dma((n_send,)),
            dma((chips,)),
            dma((n_send,)),
            dma((chips,)),
            dma((5,)),
            dma((5,)),
        ],
        compiler_params=pltpu.CompilerParams(
            collective_id=0, has_side_effects=True, vmem_limit_bytes=56 * 1024 * 1024
        ),
    )(
        fields,
        inv_jacobian.reshape(1, elements),
        face_interp.reshape(faces * nq, nodes),
        diff_matrix.reshape(3 * nodes, nodes),
        lift_matrix.transpose(0, 2, 1),
        flux_couple,
        neighbours,
        send_index,
        bound_coef,
        current_coef,
        time_interp.reshape(1, nt),
        current_history,
        group_weight,
        projection,
        kernels.reshape(pairs, nt),
        pair_dest.reshape(pairs),
        pair_count,
    )


def solution(mesh):
    both = ("patch", "level")
    placed = (
        P(None, None, both),
        P(both),
        P(),
        P(),
        P(),
        P(),
        P(None, both),
        P(None, both),
        P(),
        P(),
        P(),
        P(None, both),
        P(None, both),
        P(both, None),
        P("level", "patch", None, None),
        P("level", "patch", None),
        P("level", "patch"),
    )
    return jax.shard_map(
        per_device,
        mesh=mesh,
        in_specs=placed,
        out_specs=(P(None, None, both), P(None, both)),
        check_vma=False,
    )
```
